128 devices in a mesh: row: 4 (over z), col: 4 (over y), depth: 8 (over x, core).
Axes of the slice: x: 4, y: 4, z: 4, core: 2. Of those that a mesh axis runs over, the one named last changes fastest.
Arguments:
- tokens: bfloat16 [8, 512, 6144], P('depth', 'col', 'row'), may hold values from -6 to 6
- w_qkv: bfloat16 [3, 6144, 6144], P(None, None, ('row', 'col')), may hold values from -0.06506457 to 0.06506457
- w_out: bfloat16 [6144, 6144], P(('row', 'col')), may hold values from -0.078125 to 0.078125
- prefix: int32 [8], P('depth'), may hold values from 0 to 511
- d_out: bfloat16 [8, 512, 6144], P('depth', 'col', 'row'), may hold values from -6 to 6
Outputs:
- d_tokens: bfloat16 [8, 512, 6144], P('depth', 'col', 'row')
- d_wqkv: bfloat16 [3, 6144, 6144], P(None, 'depth', ('row', 'col'))
- d_wout: bfloat16 [6144, 6144], P(('row', 'col'), 'depth')
The draws below stay inside these ranges and needn't reach their ends.
All inputs are finite; a program needn't handle non-finite values.
Results may differ from the reference program's by a relative error of at most 0.035.
Values may be sent and summed in bfloat16 or wider, within the bound.
No kernel may reach another device: no remote copies, remote signals or barrier semaphores. Data moves between devices by JAX's collectives and lax.ppermute only.
A program may use at most 128 MiB of HBM per device.

```python
import jax
import jax.numpy as jnp
from jax import lax

D = 6144
HEADS = 48
HEAD = 128
F = 6144
L = 512
NSEQ = 8
N_ROW = 4
N_COL = 4


def draw_tokens(key, part):
    key = jax.random.fold_in(key, 3)
    key_noise = jax.random.fold_in(key, 0)
    jitter = jax.random.truncated_normal(key_noise, -6.0, 6.0, (NSEQ, L, D), jnp.float32)
    result = jitter
    return result.astype(jnp.bfloat16)


def draw_w_qkv(key, part):
    key = jax.random.fold_in(key, 5)
    key_base = jax.random.fold_in(key, 0)
    weights = jax.random.truncated_normal(key_base, -4.0, 4.0, (3, D, F), jnp.float32) * D ** (-0.5)
    return weights.astype(jnp.bfloat16)


def plant(entries, stream_key, least, largest):
    shape = entries.shape
    index_at = [jax.random.randint(jax.random.fold_in(stream_key, axis), (), 0, shape[axis]) for axis in range(len(shape))]
    entries = entries.at[tuple(index_at)].set(least)
    longest = shape.index(max(shape))
    index_at[longest] = (index_at[longest] + 1) % shape[longest]
    return entries.at[tuple(index_at)].set(largest)


def levels(key, dims, pieces, low, top_value):
    level, own = 1.0, jax.random.fold_in(key, 6)
    for dim, blocks in pieces:
        heights = jnp.exp(jax.random.uniform(jax.random.fold_in(own, dim), (blocks,), jnp.float32, low / len(pieces), top_value / len(pieces)))
        level = level * jnp.repeat(heights, dims[dim] // blocks).reshape([-1 if axis == dim else 1 for axis in range(len(dims))])
    return level


def normal_values(stream_key, extent, spread, reach, pieces=(), kind=jnp.bfloat16):
    values = spread * jax.random.normal(stream_key, extent, jnp.float32)
    if pieces:
        values = values * levels(stream_key, extent, pieces, -0.22, 0.18)
    return jnp.clip(values, -reach, reach).astype(kind)


def setup_inputs(seed: int = 0) -> dict:
    keys = jax.random.split(jax.random.key(seed), 6)
    return {
        "tokens": draw_tokens(jax.random.fold_in(keys[5], 71), 0),
        "w_qkv": draw_w_qkv(jax.random.fold_in(keys[5], 71), 0),
        "w_out": normal_values(keys[2], (F, D), F ** -0.5, 0.078125, ((0, 16),)),
        "prefix": plant(jax.random.randint(keys[3], (NSEQ,), 0, L), jax.random.fold_in(keys[3], 1), 0, L - 1).astype(jnp.int32),
        "d_out": normal_values(keys[4], (NSEQ, L, D), 1.0, 6.0, ((0, 8), (1, 4), (2, 4))),
    }


def attend(queries, keys_all, start_limit, score_scale):
    seq_len = queries.shape[0]
    position = jnp.arange(seq_len, dtype=jnp.int32)
    visible = (position[None, :] <= position[:, None]) | (position[None, :] < start_limit)
    scores = jnp.einsum("ihd,jhd->hij", queries.astype(jnp.float32), keys_all.astype(jnp.float32)) * score_scale
    scores = jnp.where(visible[None], scores, jnp.float32(-1e30))
    return jax.nn.softmax(scores, axis=-1)


def round_term(term):
    return lax.optimization_barrier(term.astype(jnp.bfloat16)).astype(jnp.float32)


def reference(tokens, w_qkv, w_out, prefix, d_out):
    groups = N_ROW * N_COL
    group_cols = F // groups
    score_scale = HEAD ** -0.5
    w_wide = w_qkv.astype(jnp.float32)
    w_group = w_wide.reshape(3, D, groups, group_cols)

    def one_sequence(carry, items):
        qkv_sum, out_sum = carry
        x_seq, dy_seq, start_limit = items
        x_wide = x_seq.astype(jnp.float32)
        qkv_all = jnp.einsum("tk,gkf->tgf", x_wide, w_wide).astype(jnp.bfloat16)
        qkv_all = qkv_all.reshape(L, 3, HEADS, HEAD)
        queries = qkv_all[:, 0]
        keys_all = qkv_all[:, 1]
        values_all = qkv_all[:, 2]
        probs = attend(queries, keys_all, start_limit, score_scale)
        probs_half = probs.astype(jnp.bfloat16)
        context = jnp.einsum("hij,jhd->ihd", probs_half.astype(jnp.float32), values_all.astype(jnp.float32)).astype(jnp.bfloat16)
        context_flat = context.reshape(L, F)
        d_context = jnp.dot(dy_seq, w_out.T, preferred_element_type=jnp.float32).astype(jnp.bfloat16)
        d_context = d_context.reshape(L, HEADS, HEAD).astype(jnp.float32)
        out_term = jnp.dot(context_flat.T, dy_seq, preferred_element_type=jnp.float32)
        d_values = jnp.einsum("hij,ihd->jhd", probs_half.astype(jnp.float32), d_context).astype(jnp.bfloat16)
        d_probs = jnp.einsum("ihd,jhd->hij", d_context, values_all.astype(jnp.float32))
        d_scores = (probs * (d_probs - jnp.sum(probs * d_probs, axis=-1, keepdims=True)) * score_scale).astype(jnp.bfloat16)
        d_queries = jnp.einsum("hij,jhd->ihd", d_scores.astype(jnp.float32), keys_all.astype(jnp.float32)).astype(jnp.bfloat16)
        d_keys = jnp.einsum("hij,ihd->jhd", d_scores.astype(jnp.float32), queries.astype(jnp.float32)).astype(jnp.bfloat16)
        d_qkv = jnp.stack((d_queries, d_keys, d_values), axis=1).reshape(L, 3, F).astype(jnp.float32)
        input_terms = jnp.einsum("tegf,ekgf->gtk", d_qkv.reshape(L, 3, groups, group_cols), w_group)
        d_tokens = jnp.sum(round_term(input_terms), axis=0).astype(jnp.bfloat16)
        qkv_term = jnp.einsum("tk,tef->ekf", x_wide, d_qkv)
        return (qkv_sum + round_term(qkv_term), out_sum + round_term(out_term)), d_tokens

    start = (jnp.zeros((3, D, F), jnp.float32), jnp.zeros((F, D), jnp.float32))
    sums, d_tokens = lax.scan(one_sequence, start, (tokens, d_out, prefix))
    return d_tokens, sums[0].astype(jnp.bfloat16), sums[1].astype(jnp.bfloat16)
```

```python
import functools

import jax
import jax.numpy as jnp
from jax import lax
from jax.experimental import pallas as pl
from jax.experimental.pallas import tpu as pltpu
from jax.sharding import PartitionSpec as P

HEAD = 128
SIDE = 4
BF = jnp.bfloat16
F32 = jnp.float32


def dot(a, b, ca, cb):
    return lax.dot_general(a, b, (((ca,), (cb,)), ((), ())), preferred_element_type=F32)


def duo(x, axis, k):
    if axis == "depth":
        pairs = [(d, (d + (2 * k if d % 2 == 0 else -2 * k)) % 8) for d in range(8)]
        return lax.ppermute(x, "depth", pairs)
    pairs = [
        (i * 8 + d, ((i + (k if d % 2 == 0 else -k)) % SIDE) * 8 + d)
        for i in range(SIDE)
        for d in range(8)
    ]
    return lax.ppermute(x, (axis, "depth"), pairs)


def swap_cores(x):
    return lax.ppermute(x, "depth", [(d, d ^ 1) for d in range(8)])


def params(mib):
    return pltpu.CompilerParams(vmem_limit_bytes=mib * 1024 * 1024)


def ordered(kernel, outs, in_specs, out_specs, scratch, after, prefetch=0, **kw):
    n_in, n_out = len(in_specs) + prefetch, len(outs)

    def with_order(*refs):
        kernel(*refs[:n_in], *refs[n_in + 1 : n_in + 1 + n_out], *refs[n_in + 2 + n_out :])

    anywhere = pl.BlockSpec(memory_space=pltpu.HBM)
    outs = list(outs) + [jax.ShapeDtypeStruct((8, 128), F32)]
    in_specs, out_specs = list(in_specs) + [anywhere], list(out_specs) + [anywhere]
    if prefetch:
        kw["grid_spec"] = pltpu.PrefetchScalarGridSpec(
            num_scalar_prefetch=prefetch,
            grid=kw.pop("grid"),
            in_specs=in_specs,
            out_specs=out_specs,
            scratch_shapes=scratch,
        )
    else:
        kw.update(in_specs=in_specs, out_specs=out_specs, scratch_shapes=scratch)
    return lambda *args: pl.pallas_call(with_order, out_shape=outs, **kw)(*args, after)


def cost(flops, nbytes):
    return pl.CostEstimate(flops=flops, bytes_accessed=nbytes, transcendentals=0)


def part_kernel(turn, contract, idx, mine, wm, *rest):
    pair = turn % 2
    if pair:
        others, wo, rest = rest[:2], rest[2], rest[3:]
    acc_in = rest[0] if turn else None
    out, acc = rest[-2:]
    step = pl.program_id(0)

    def weights(w):
        if w.ndim == 5:
            return jnp.concatenate([w[g, 0, 0] for g in range(3)], axis=1)
        return w[...]

    @pl.when(step == 0)
    def _():
        value = dot(mine[...], weights(wm), 1, contract)
        acc[...] = value + acc_in[...] if turn else value

    if pair:
        rows = jnp.concatenate([v[0] for v in others], axis=0)
        block = others[0].shape[1]
        acc[(turn - 1) * block : (turn + 1) * block, :] += dot(rows, weights(wo), 1, contract)

    @pl.when(step == pl.num_programs(0) - 1)
    def _():
        out[...] = acc[...].astype(out.dtype)


def project(after, turn, idx, mine, others, w, acc):
    rows, half = mine.shape
    wide = w.ndim == 5
    if wide:
        cols = 3 * w.shape[-1]
        w_block = (3, 1, 1, half, w.shape[-1])
        w_mine = pl.BlockSpec(w_block, lambda j, s: (0, s[turn], s[4], 0, 0))
        w_other = pl.BlockSpec(w_block, lambda j, s: (0, s[j], 1 - s[4], 0, 0))
    else:
        cols = w.shape[0]
        w_mine = pl.BlockSpec((cols, half), lambda j, s: (0, 2 * s[turn] + s[4]))
        w_other = pl.BlockSpec((cols, half), lambda j, s: (0, 2 * s[j] + 1 - s[4]))
    whole = pl.BlockSpec((rows, cols), lambda j, s: (0, 0))
    specs, args = [pl.BlockSpec((rows, half), lambda j, s: (0, 0)), w_mine], [mine, w]
    if turn % 2:
        block = others[0].shape[1]
        specs += [pl.BlockSpec((1, block, half), lambda j, s: (j, 0, 0))] * 2 + [w_other]
        args += others[turn - 1 : turn + 1] + [w]
    if turn:
        specs.append(whole)
        args.append(acc)
    last = turn == SIDE - 1
    return ordered(
        functools.partial(part_kernel, turn, 0 if wide else 1),
        [jax.ShapeDtypeStruct((rows, cols), BF if last else F32)],
        specs,
        [whole],
        [pltpu.VMEM((rows, cols), F32)],
        after,
        prefetch=1,
        grid=(SIDE if turn % 2 else 1,),
        compiler_params=params(48),
        cost_estimate=cost(4 * rows * half * cols, 16_000_000),
        name="project_qkv" if wide else "project_dctx",
    )(idx, *args)


def probs_t(queries, keys, visible, scale):
    scores = jnp.where(visible, dot(keys, queries, 1, 1) * scale, F32(-1e30))
    top = jnp.max(scores, axis=0, keepdims=True)
    e = jnp.exp(scores - top)
    return e / jnp.sum(e, axis=0, keepdims=True)


def split_heads(ref, cols, h):
    return [ref[:, g * cols + h * HEAD : g * cols + (h + 1) * HEAD] for g in range(3)]


def attend_kernel(prefix, qkv, pos_col, pos_row, out):
    cols = out.shape[0]
    key_pos, query_pos = pos_col[...], pos_row[...]
    visible = (key_pos <= query_pos) | (key_pos < prefix[0])
    for h in range(cols // HEAD):
        q, k, v = split_heads(qkv, cols, h)
        probs = probs_t(q, k, visible, HEAD ** (-0.5))
        out[h * HEAD : (h + 1) * HEAD, :] = dot(v, probs.astype(BF), 0, 0).astype(BF)


def attend(after, prefix, qkv, pos_col, pos_row):
    rows, cols = qkv.shape[0], qkv.shape[1] // 3
    vm = pl.BlockSpec(memory_space=pltpu.VMEM)
    return ordered(
        attend_kernel,
        [jax.ShapeDtypeStruct((cols, rows), BF)],
        [pl.BlockSpec(memory_space=pltpu.SMEM), vm, vm, vm],
        [vm],
        [],
        after,
        compiler_params=params(16),
        cost_estimate=cost(4 * rows * rows * cols, 2_000_000),
        name="attend",
    )(prefix, qkv, pos_col, pos_row)


def back_kernel(prefix, qkv, d_ctx, pos_col, pos_row, out):
    cols = d_ctx.shape[1]
    scale = HEAD ** (-0.5)
    key_pos, query_pos = pos_col[...], pos_row[...]
    visible = (key_pos <= query_pos) | (key_pos < prefix[0])
    for h in range(cols // HEAD):
        q, k, v = split_heads(qkv, cols, h)
        dc = d_ctx[:, h * HEAD : (h + 1) * HEAD]
        probs = probs_t(q, k, visible, scale)
        d_probs = dot(v, dc, 1, 1)
        total = jnp.sum(probs * d_probs, axis=0, keepdims=True)
        ds = (probs * (d_probs - total) * scale).astype(BF)
        d_v = dot(probs.astype(BF), dc, 1, 0)
        d_k = dot(ds, q, 1, 0)
        d_q = dot(k, ds, 0, 0).T
        for g, val in enumerate((d_q, d_k, d_v)):
            out[:, g * cols + h * HEAD : g * cols + (h + 1) * HEAD] = val.astype(BF)


def attend_back(after, prefix, qkv, d_ctx, pos_col, pos_row):
    rows, cols = d_ctx.shape
    vm = pl.BlockSpec(memory_space=pltpu.VMEM)
    return ordered(
        back_kernel,
        [jax.ShapeDtypeStruct((rows, 3 * cols), BF)],
        [pl.BlockSpec(memory_space=pltpu.SMEM), vm, vm, vm, vm],
        [vm],
        [],
        after,
        compiler_params=params(20),
        cost_estimate=cost(10 * rows * rows * cols, 3_000_000),
        name="attend_back",
    )(prefix, qkv, d_ctx, pos_col, pos_row)


def input_kernel(idx, dq, w, out):
    wide = jnp.concatenate([w[g, 0, 0] for g in range(3)], axis=1)
    out[...] = dot(dq[...], wide, 1, 1).astype(BF).reshape(out.shape)


def input_terms(after, mine, idx, dq, w5, block):
    rows = dq.shape[0]
    half, cols = w5.shape[-2:]
    if mine:
        shape = (SIDE, rows, half)
        out_spec = pl.BlockSpec((1, rows, half), lambda j, s: (j, 0, 0))
        w_spec = pl.BlockSpec((3, 1, 1, half, cols), lambda j, s: (0, s[j], s[4], 0, 0))
    else:
        shape = (SIDE, SIDE, block, half)
        out_spec = pl.BlockSpec((SIDE, 1, block, half), lambda j, s: (0, j, 0, 0))
        w_spec = pl.BlockSpec((3, 1, 1, half, cols), lambda j, s: (0, s[j], 1 - s[4], 0, 0))
    return ordered(
        input_kernel,
        [jax.ShapeDtypeStruct(shape, BF)],
        [pl.BlockSpec((rows, 3 * cols), lambda j, s: (0, 0)), w_spec],
        [out_spec],
        [],
        after,
        prefetch=1,
        grid=(SIDE,),
        compiler_params=params(48),
        cost_estimate=cost(2 * rows * SIDE * half * 3 * cols, 11_000_000),
        name="input_terms",
    )(idx, dq, w5)


def fetch(idx, slot, at, mine, pair, mine_v, pair_v, sems):
    width = mine_v.shape[-1]
    lanes = pl.ds(at * width, width)
    for j in range(SIDE):

        @pl.when(idx[5 + slot] == j)
        def _():
            pltpu.make_async_copy(mine[j].at[:, lanes], mine_v, sems.at[SIDE]).start()

    block = pair_v.shape[0] // SIDE
    copies = [pltpu.make_async_copy(mine[0].at[:, lanes], mine_v, sems.at[SIDE])]
    for i in range(SIDE):
        src = pair[i].at[idx[9 + slot], :, lanes]
        copy = pltpu.make_async_copy(src, pair_v.at[i * block : (i + 1) * block], sems.at[i])
        copy.start()
        copies.append(copy)
    return copies


def chunk_kernel(slot, at, wide, n_add, idx, *refs):
    mine, pair, (own, own_p) = refs[:SIDE], refs[SIDE : 2 * SIDE], refs[2 * SIDE : 2 * SIDE + 2]
    rest = refs[2 * SIDE + 2 :]
    incoming, (out, mine_v, pair_v, sems) = rest[:n_add], rest[n_add:]
    for copy in fetch(idx, slot, at, mine, pair, mine_v, pair_v, sems):
        copy.wait()
    if not wide:
        total = dot(own[...], mine_v[...], 1, 0) + dot(own_p[...], pair_v[...], 1, 0)
        for v in incoming:
            total += v[...].astype(F32)
        out[...] = total.astype(BF)
        return
    cols = out.shape[-1]
    total = dot(mine_v[...], own[...], 0, 0) + dot(pair_v[...], own_p[...], 0, 0)
    rows = out.shape[1] // max(n_add, 1)
    for g in range(3):
        part = total[:, g * cols : (g + 1) * cols]
        if not n_add:
            out[g] = part.astype(BF)
        for u in range(n_add):
            sl = slice(u * rows, (u + 1) * rows)
            out[g, sl, :] = (part[sl] + incoming[u][g].astype(F32)).astype(BF)


def chunk(after, slot, sub, idx, mine, pair, own, own_p, incoming):
    rows, half = mine[0].shape
    wide = own.shape[0] == rows
    width = half if sub is None else half // 2
    cols = own.shape[1] // 3 if wide else own.shape[0]
    shape = (3, width, cols) if wide else (cols, width)
    anywhere = pl.BlockSpec(memory_space=pltpu.HBM)
    vm = pl.BlockSpec(memory_space=pltpu.VMEM)
    return ordered(
        functools.partial(chunk_kernel, slot, sub or 0, wide, len(incoming)),
        [jax.ShapeDtypeStruct(shape, BF)],
        [pl.BlockSpec(memory_space=pltpu.SMEM)]
        + [anywhere] * (2 * SIDE)
        + [vm] * (2 + len(incoming)),
        [vm],
        [
            pltpu.VMEM((rows, width), BF),
            pltpu.VMEM((rows, width), BF),
            pltpu.SemaphoreType.DMA((SIDE + 1,)),
        ],
        after,
        compiler_params=params(24),
        cost_estimate=cost(4 * rows * width * cols * (3 if wide else 1), 5_000_000),
        name="wqkv_chunk" if wide else "wout_chunk",
    )(idx, *mine, *pair, own, own_p, *incoming)


def spread(mine, other):
    m = [mine] + [duo(mine, "col", k) for k in (1, 2, 3)]
    o = [other] + [duo(other, "row", k) for k in (1, 2, 3)]
    return jnp.stack(m), jnp.stack(o)


def hold(values, after):
    return lax.optimization_barrier((values, after))[0]


def add_kernel(a, b, out):
    out[...] = (a[...].astype(F32) + b[0].astype(F32)).astype(BF)


def add(after, got, terms, j):
    whole = pl.BlockSpec(got.shape, lambda i: (0, 0, 0))
    return ordered(
        add_kernel,
        [jax.ShapeDtypeStruct(got.shape, BF)],
        [whole, pl.BlockSpec((1, *got.shape), lambda i: (j, 0, 0, 0))],
        [whole],
        [],
        after,
        grid=(1,),
        compiler_params=params(16),
        name="add_term",
    )(got, terms)


def finish(s, axis):
    got = [duo(s[i], axis, -i) for i in (1, 2, 3)]
    return sum((v.astype(F32) for v in got), s[0].astype(F32)).astype(BF)


def body(tokens, w_qkv, w_out, prefix, d_out):
    block, width = tokens.shape[1], tokens.shape[2]
    half = width // 2
    cols = w_qkv.shape[2]
    z, y = lax.axis_index("row"), lax.axis_index("col")
    depth = lax.axis_index("depth")
    core = depth % 2
    x = depth // 2
    sign = 1 - 2 * core
    steps = jnp.arange(SIDE, dtype=jnp.int32)
    owner_row = (z - sign * steps) % SIDE
    owner_col = (y - sign * steps) % SIDE
    targets = (x - sign * jnp.array([1, 2, 3, 0], jnp.int32)) % SIDE
    own_slot = (sign * (z - targets)) % SIDE
    pair_slot = (-own_slot) % SIDE
    idx = jnp.concatenate([owner_row, core[None], own_slot, pair_slot, owner_col]).astype(jnp.int32)
    pos = (owner_col[:, None] * block + jnp.arange(block, dtype=jnp.int32)[None]).reshape(-1)
    pos_col, pos_row = pos[:, None], pos[None, :]
    w5 = w_qkv.reshape(3, SIDE, 2, half, cols)

    def halves(v):
        return (
            lax.dynamic_slice(v[0], (0, core * half), (block, half)),
            lax.dynamic_slice(v[0], (0, (1 - core) * half), (block, half)),
        )

    def flat(v):
        return v.reshape(-1, half)

    order = jnp.zeros((8, 128), F32)
    xs = [spread(*halves(tokens))]
    ys = [spread(*hold(halves(d_out), xs[0]))]
    qkv = d_ctx = None
    xp, yp = [], []

    def pass_on(sets, pairs):
        m, o = sets[-1]
        pairs.append(swap_cores(o))
        sets.append((duo(m, "row", 1), duo(o, "col", 1)))

    for turn in range(SIDE - 1):
        if turn:
            (xs[turn], xp[-1]), order = lax.optimization_barrier(((xs[turn], xp[-1]), order))
        pass_on(xs, xp)
        qkv, order = project(order, turn, idx, flat(xs[turn][0]), [v[1] for v in xs], w5, qkv)
        if turn:
            (ys[turn], yp[-1]), order = lax.optimization_barrier(((ys[turn], yp[-1]), order))
        pass_on(ys, yp)
        d_ctx, order = project(order, turn, idx, flat(ys[turn][0]), [v[1] for v in ys], w_out, d_ctx)
    turn = SIDE - 1
    xm, ym = [flat(v[0]) for v in xs], [flat(v[0]) for v in ys]
    xp.append(swap_cores(xs[turn][1]))
    yp.append(swap_cores(ys[turn][1]))
    qkv, order = project(order, turn, idx, xm[turn], [v[1] for v in xs], w5, qkv)
    ctx, order = attend(order, prefix, qkv, pos_col, pos_row)
    ctx_p = swap_cores(ctx)
    d_ctx, order = project(order, turn, idx, ym[turn], [v[1] for v in ys], w_out, d_ctx)
    d_qkv, order = attend_back(order, prefix, qkv, d_ctx, pos_col, pos_row)
    d_qkv_p = swap_cores(d_qkv)

    def out_chunk(order, slot, incoming):
        v, order = chunk(order, slot, None, idx, ym, yp, ctx, ctx_p, incoming)
        return v if slot == SIDE - 1 else duo(v, "depth", 1), order

    def qkv_chunk(order, slot, sub, incoming):
        v, order = chunk(order, slot, sub, idx, xm, xp, d_qkv, d_qkv_p, incoming)
        return v if slot == SIDE - 1 else duo(v, "depth", 1), order

    out, order = out_chunk(order, 0, [])
    term_m, order = input_terms(order, True, idx, d_qkv, w5, block)
    term_m = term_m.reshape(SIDE, SIDE, block, half)
    m = duo(term_m[1], "row", 1)
    sub0, order = qkv_chunk(order, 0, 0, [])
    sub1, order = qkv_chunk(order, 0, 1, [])
    term_o, order = input_terms(order, False, idx, d_qkv, w5, block)
    o = duo(term_o[1], "col", 1)
    out, order = out_chunk(order, 1, [out])
    m, order = add(order, m, term_m, 2)
    m = duo(m, "row", 1)
    sub0, order = qkv_chunk(order, 1, 0, [sub0])
    o, order = add(order, o, term_o, 2)
    o = duo(o, "col", 1)
    sub1, order = qkv_chunk(order, 1, 1, [sub1])
    m, order = add(order, m, term_m, 3)
    m = duo(m, "row", 1)
    out, order = out_chunk(order, 2, [out])
    o, order = add(order, o, term_o, 3)
    o = duo(o, "col", 1)
    sub0, order = qkv_chunk(order, 2, 0, [sub0])
    m, order = add(order, m, term_m, 0)
    sub1, order = qkv_chunk(order, 2, 1, [sub1])
    o, order = add(order, o, term_o, 0)
    part_m, part_o = finish(m, "col"), finish(o, "row")
    d_wout, order = out_chunk(order, 3, [out])
    d_wqkv, order = qkv_chunk(order, 3, None, [sub0, sub1])
    d_tokens = jnp.where(
        core == 0,
        jnp.concatenate([part_m, part_o], axis=1),
        jnp.concatenate([part_o, part_m], axis=1),
    )[None]
    return (d_tokens, d_wqkv, d_wout)


def solution(mesh):
    in_specs = (
        P("depth", "col", "row"),
        P(None, None, ("row", "col")),
        P(("row", "col"), None),
        P("depth"),
        P("depth", "col", "row"),
    )
    out_specs = (
        P("depth", "col", "row"),
        P(None, "depth", ("row", "col")),
        P(("row", "col"), "depth"),
    )
    return jax.shard_map(body, mesh=mesh, in_specs=in_specs, out_specs=out_specs, check_vma=False)
```

```python
import functools

import jax
import jax.numpy as jnp
from jax import lax
from jax.experimental import pallas as pl
from jax.experimental.pallas import tpu as pltpu
from jax.sharding import PartitionSpec as P

HEAD = 128
SIDE = 4
BF = jnp.bfloat16
F32 = jnp.float32


def dot(a, b, ca, cb):
    return lax.dot_general(a, b, (((ca,), (cb,)), ((), ())), preferred_element_type=F32)


def duo(x, axis, k):
    if axis == "depth":
        pairs = [(d, (d + (2 * k if d % 2 == 0 else -2 * k)) % 8) for d in range(8)]
        return lax.ppermute(x, "depth", pairs)
    pairs = [
        (i * 8 + d, ((i + (k if d % 2 == 0 else -k)) % SIDE) * 8 + d)
        for i in range(SIDE)
        for d in range(8)
    ]
    return lax.ppermute(x, (axis, "depth"), pairs)


def swap_cores(x):
    return lax.ppermute(x, "depth", [(d, d ^ 1) for d in range(8)])


def params(mib):
    return pltpu.CompilerParams(vmem_limit_bytes=mib * 1024 * 1024)


def ordered(kernel, outs, in_specs, out_specs, scratch, after, prefetch=0, **kw):
    n_in, n_out = len(in_specs) + prefetch, len(outs)

    def with_order(*refs):
        kernel(*refs[:n_in], *refs[n_in + 1 : n_in + 1 + n_out], *refs[n_in + 2 + n_out :])

    anywhere = pl.BlockSpec(memory_space=pltpu.HBM)
    outs = list(outs) + [jax.ShapeDtypeStruct((8, 128), F32)]
    in_specs, out_specs = list(in_specs) + [anywhere], list(out_specs) + [anywhere]
    if prefetch:
        kw["grid_spec"] = pltpu.PrefetchScalarGridSpec(
            num_scalar_prefetch=prefetch,
            grid=kw.pop("grid"),
            in_specs=in_specs,
            out_specs=out_specs,
            scratch_shapes=scratch,
        )
    else:
        kw.update(in_specs=in_specs, out_specs=out_specs, scratch_shapes=scratch)
    return lambda *args: pl.pallas_call(with_order, out_shape=outs, **kw)(*args, after)


def cost(flops, nbytes):
    return pl.CostEstimate(flops=flops, bytes_accessed=nbytes, transcendentals=0)


def part_kernel(turn, contract, idx, mine, wm, *rest):
    pair = turn % 2
    if pair:
        others, wo, rest = rest[:2], rest[2], rest[3:]
    acc_in = rest[0] if turn else None
    out, acc = rest[-2:]
    step = pl.program_id(0)

    def weights(w):
        if w.ndim == 5:
            return jnp.concatenate([w[g, 0, 0] for g in range(3)], axis=1)
        return w[...]

    @pl.when(step == 0)
    def _():
        value = dot(mine[...], weights(wm), 1, contract)
        acc[...] = value + acc_in[...] if turn else value

    if pair:
        rows = jnp.concatenate([v[0] for v in others], axis=0)
        block = others[0].shape[1]
        acc[(turn - 1) * block : (turn + 1) * block, :] += dot(rows, weights(wo), 1, contract)

    @pl.when(step == pl.num_programs(0) - 1)
    def _():
        out[...] = acc[...].astype(out.dtype)


def project(after, turn, idx, mine, others, w, acc):
    rows, half = mine.shape
    wide = w.ndim == 5
    if wide:
        cols = 3 * w.shape[-1]
        w_block = (3, 1, 1, half, w.shape[-1])
        w_mine = pl.BlockSpec(w_block, lambda j, s: (0, s[turn], s[4], 0, 0))
        w_other = pl.BlockSpec(w_block, lambda j, s: (0, s[j], 1 - s[4], 0, 0))
    else:
        cols = w.shape[0]
        w_mine = pl.BlockSpec((cols, half), lambda j, s: (0, 2 * s[turn] + s[4]))
        w_other = pl.BlockSpec((cols, half), lambda j, s: (0, 2 * s[j] + 1 - s[4]))
    whole = pl.BlockSpec((rows, cols), lambda j, s: (0, 0))
    specs, args = [pl.BlockSpec((rows, half), lambda j, s: (0, 0)), w_mine], [mine, w]
    if turn % 2:
        block = others[0].shape[1]
        specs += [pl.BlockSpec((1, block, half), lambda j, s: (j, 0, 0))] * 2 + [w_other]
        args += others[turn - 1 : turn + 1] + [w]
    if turn:
        specs.append(whole)
        args.append(acc)
    last = turn == SIDE - 1
    return ordered(
        functools.partial(part_kernel, turn, 0 if wide else 1),
        [jax.ShapeDtypeStruct((rows, cols), BF if last else F32)],
        specs,
        [whole],
        [pltpu.VMEM((rows, cols), F32)],
        after,
        prefetch=1,
        grid=(SIDE if turn % 2 else 1,),
        compiler_params=params(48),
        cost_estimate=cost(4 * rows * half * cols, 16_000_000),
        name="project_qkv" if wide else "project_dctx",
    )(idx, *args)


def probs_t(queries, keys, visible, scale):
    scores = jnp.where(visible, dot(keys, queries, 1, 1) * scale, F32(-1e30))
    top = jnp.max(scores, axis=0, keepdims=True)
    e = jnp.exp(scores - top)
    return e / jnp.sum(e, axis=0, keepdims=True)


def split_heads(ref, cols, h):
    return [ref[:, g * cols + h * HEAD : g * cols + (h + 1) * HEAD] for g in range(3)]


def attend_kernel(prefix, qkv, pos_col, pos_row, out):
    cols = out.shape[0]
    key_pos, query_pos = pos_col[...], pos_row[...]
    visible = (key_pos <= query_pos) | (key_pos < prefix[0])
    for h in range(cols // HEAD):
        q, k, v = split_heads(qkv, cols, h)
        probs = probs_t(q, k, visible, HEAD ** (-0.5))
        out[h * HEAD : (h + 1) * HEAD, :] = dot(v, probs.astype(BF), 0, 0).astype(BF)


def attend(after, prefix, qkv, pos_col, pos_row):
    rows, cols = qkv.shape[0], qkv.shape[1] // 3
    vm = pl.BlockSpec(memory_space=pltpu.VMEM)
    return ordered(
        attend_kernel,
        [jax.ShapeDtypeStruct((cols, rows), BF)],
        [pl.BlockSpec(memory_space=pltpu.SMEM), vm, vm, vm],
        [vm],
        [],
        after,
        compiler_params=params(16),
        cost_estimate=cost(4 * rows * rows * cols, 2_000_000),
        name="attend",
    )(prefix, qkv, pos_col, pos_row)


def back_kernel(prefix, qkv, d_ctx, pos_col, pos_row, out):
    cols = d_ctx.shape[1]
    scale = HEAD ** (-0.5)
    key_pos, query_pos = pos_col[...], pos_row[...]
    visible = (key_pos <= query_pos) | (key_pos < prefix[0])
    for h in range(cols // HEAD):
        q, k, v = split_heads(qkv, cols, h)
        dc = d_ctx[:, h * HEAD : (h + 1) * HEAD]
        probs = probs_t(q, k, visible, scale)
        d_probs = dot(v, dc, 1, 1)
        total = jnp.sum(probs * d_probs, axis=0, keepdims=True)
        ds = (probs * (d_probs - total) * scale).astype(BF)
        d_v = dot(probs.astype(BF), dc, 1, 0)
        d_k = dot(ds, q, 1, 0)
        d_q = dot(k, ds, 0, 0).T
        for g, val in enumerate((d_q, d_k, d_v)):
            out[:, g * cols + h * HEAD : g * cols + (h + 1) * HEAD] = val.astype(BF)


def attend_back(after, prefix, qkv, d_ctx, pos_col, pos_row):
    rows, cols = d_ctx.shape
    vm = pl.BlockSpec(memory_space=pltpu.VMEM)
    return ordered(
        back_kernel,
        [jax.ShapeDtypeStruct((rows, 3 * cols), BF)],
        [pl.BlockSpec(memory_space=pltpu.SMEM), vm, vm, vm, vm],
        [vm],
        [],
        after,
        compiler_params=params(20),
        cost_estimate=cost(10 * rows * rows * cols, 3_000_000),
        name="attend_back",
    )(prefix, qkv, d_ctx, pos_col, pos_row)


def input_kernel(idx, dq, w, out):
    wide = jnp.concatenate([w[g, 0, 0] for g in range(3)], axis=1)
    out[...] = dot(dq[...], wide, 1, 1).astype(BF).reshape(out.shape)


def input_terms(after, mine, idx, dq, w5, block):
    rows = dq.shape[0]
    half, cols = w5.shape[-2:]
    if mine:
        shape = (SIDE, rows, half)
        out_spec = pl.BlockSpec((1, rows, half), lambda j, s: (j, 0, 0))
        w_spec = pl.BlockSpec((3, 1, 1, half, cols), lambda j, s: (0, s[j], s[4], 0, 0))
    else:
        shape = (SIDE, SIDE, block, half)
        out_spec = pl.BlockSpec((SIDE, 1, block, half), lambda j, s: (0, j, 0, 0))
        w_spec = pl.BlockSpec((3, 1, 1, half, cols), lambda j, s: (0, s[j], 1 - s[4], 0, 0))
    return ordered(
        input_kernel,
        [jax.ShapeDtypeStruct(shape, BF)],
        [pl.BlockSpec((rows, 3 * cols), lambda j, s: (0, 0)), w_spec],
        [out_spec],
        [],
        after,
        prefetch=1,
        grid=(SIDE,),
        compiler_params=params(48),
        cost_estimate=cost(2 * rows * SIDE * half * 3 * cols, 11_000_000),
        name="input_terms",
    )(idx, dq, w5)


def fetch(idx, slot, at, mine, pair, mine_v, pair_v, sems):
    width = mine_v.shape[-1]
    lanes = pl.ds(at * width, width)
    for j in range(SIDE):

        @pl.when(idx[5 + slot] == j)
        def _():
            pltpu.make_async_copy(mine[j].at[:, lanes], mine_v, sems.at[SIDE]).start()

    block = pair_v.shape[0] // SIDE
    copies = [pltpu.make_async_copy(mine[0].at[:, lanes], mine_v, sems.at[SIDE])]
    for i in range(SIDE):
        src = pair[i].at[idx[9 + slot], :, lanes]
        copy = pltpu.make_async_copy(src, pair_v.at[i * block : (i + 1) * block], sems.at[i])
        copy.start()
        copies.append(copy)
    return copies


def chunk_kernel(slot, at, wide, n_add, idx, *refs):
    mine, pair, (own, own_p) = refs[:SIDE], refs[SIDE : 2 * SIDE], refs[2 * SIDE : 2 * SIDE + 2]
    rest = refs[2 * SIDE + 2 :]
    incoming, (out, mine_v, pair_v, sems) = rest[:n_add], rest[n_add:]
    for copy in fetch(idx, slot, at, mine, pair, mine_v, pair_v, sems):
        copy.wait()
    if not wide:
        total = dot(own[...], mine_v[...], 1, 0) + dot(own_p[...], pair_v[...], 1, 0)
        for v in incoming:
            total += v[...].astype(F32)
        out[...] = total.astype(BF)
        return
    cols = out.shape[-1]
    total = dot(mine_v[...], own[...], 0, 0) + dot(pair_v[...], own_p[...], 0, 0)
    rows = out.shape[1] // max(n_add, 1)
    for g in range(3):
        part = total[:, g * cols : (g + 1) * cols]
        if not n_add:
            out[g] = part.astype(BF)
        for u in range(n_add):
            sl = slice(u * rows, (u + 1) * rows)
            out[g, sl, :] = (part[sl] + incoming[u][g].astype(F32)).astype(BF)


def chunk(after, slot, sub, idx, mine, pair, own, own_p, incoming):
    rows, half = mine[0].shape
    wide = own.shape[0] == rows
    width = half if sub is None else half // 2
    cols = own.shape[1] // 3 if wide else own.shape[0]
    shape = (3, width, cols) if wide else (cols, width)
    anywhere = pl.BlockSpec(memory_space=pltpu.HBM)
    vm = pl.BlockSpec(memory_space=pltpu.VMEM)
    return ordered(
        functools.partial(chunk_kernel, slot, sub or 0, wide, len(incoming)),
        [jax.ShapeDtypeStruct(shape, BF)],
        [pl.BlockSpec(memory_space=pltpu.SMEM)]
        + [anywhere] * (2 * SIDE)
        + [vm] * (2 + len(incoming)),
        [vm],
        [
            pltpu.VMEM((rows, width), BF),
            pltpu.VMEM((rows, width), BF),
            pltpu.SemaphoreType.DMA((SIDE + 1,)),
        ],
        after,
        compiler_params=params(24),
        cost_estimate=cost(4 * rows * width * cols * (3 if wide else 1), 5_000_000),
        name="wqkv_chunk" if wide else "wout_chunk",
    )(idx, *mine, *pair, own, own_p, *incoming)


def spread(mine, other):
    m = [mine] + [duo(mine, "col", k) for k in (1, 2, 3)]
    o = [other] + [duo(other, "row", k) for k in (1, 2, 3)]
    return jnp.stack(m), jnp.stack(o)


def hold(values, after):
    return lax.optimization_barrier((values, after))[0]


def add_kernel(a, b, out):
    out[...] = (a[...].astype(F32) + b[0].astype(F32)).astype(BF)


def add(after, got, terms, j):
    whole = pl.BlockSpec(got.shape, lambda i: (0, 0, 0))
    return ordered(
        add_kernel,
        [jax.ShapeDtypeStruct(got.shape, BF)],
        [whole, pl.BlockSpec((1, *got.shape), lambda i: (j, 0, 0, 0))],
        [whole],
        [],
        after,
        grid=(1,),
        compiler_params=params(16),
        name="add_term",
    )(got, terms)


def finish(s, axis):
    got = [duo(s[i], axis, -i) for i in (1, 2, 3)]
    return sum((v.astype(F32) for v in got), s[0].astype(F32)).astype(BF)


def body(tokens, w_qkv, w_out, prefix, d_out):
    block, width = tokens.shape[1], tokens.shape[2]
    half = width // 2
    cols = w_qkv.shape[2]
    z, y = lax.axis_index("row"), lax.axis_index("col")
    depth = lax.axis_index("depth")
    core = depth % 2
    x = depth // 2
    sign = 1 - 2 * core
    steps = jnp.arange(SIDE, dtype=jnp.int32)
    owner_row = (z - sign * steps) % SIDE
    owner_col = (y - sign * steps) % SIDE
    targets = (x - sign * jnp.array([1, 2, 3, 0], jnp.int32)) % SIDE
    own_slot = (sign * (z - targets)) % SIDE
    pair_slot = (-own_slot) % SIDE
    idx = jnp.concatenate([owner_row, core[None], own_slot, pair_slot, owner_col]).astype(jnp.int32)
    pos = (owner_col[:, None] * block + jnp.arange(block, dtype=jnp.int32)[None]).reshape(-1)
    pos_col, pos_row = pos[:, None], pos[None, :]
    w5 = w_qkv.reshape(3, SIDE, 2, half, cols)

    def halves(v):
        return (
            lax.dynamic_slice(v[0], (0, core * half), (block, half)),
            lax.dynamic_slice(v[0], (0, (1 - core) * half), (block, half)),
        )

    def flat(v):
        return v.reshape(-1, half)

    order = jnp.zeros((8, 128), F32)
    xs = [spread(*halves(tokens))]
    ys = [spread(*hold(halves(d_out), xs[0]))]
    qkv = d_ctx = None
    xp, yp = [], []

    def pass_on(sets, pairs):
        m, o = sets[-1]
        pairs.append(swap_cores(o))
        sets.append((duo(m, "row", 1), duo(o, "col", 1)))

    for turn in range(SIDE - 1):
        if turn:
            (xs[turn], xp[-1]), order = lax.optimization_barrier(((xs[turn], xp[-1]), order))
        pass_on(xs, xp)
        qkv, order = project(order, turn, idx, flat(xs[turn][0]), [v[1] for v in xs], w5, qkv)
        if turn:
            (ys[turn], yp[-1]), order = lax.optimization_barrier(((ys[turn], yp[-1]), order))
        pass_on(ys, yp)
        d_ctx, order = project(order, turn, idx, flat(ys[turn][0]), [v[1] for v in ys], w_out, d_ctx)
    turn = SIDE - 1
    xm, ym = [flat(v[0]) for v in xs], [flat(v[0]) for v in ys]
    xp.append(swap_cores(xs[turn][1]))
    yp.append(swap_cores(ys[turn][1]))
    qkv, order = project(order, turn, idx, xm[turn], [v[1] for v in xs], w5, qkv)
    ctx, order = attend(order, prefix, qkv, pos_col, pos_row)
    ctx_p = swap_cores(ctx)
    d_ctx, order = project(order, turn, idx, ym[turn], [v[1] for v in ys], w_out, d_ctx)
    d_qkv, order = attend_back(order, prefix, qkv, d_ctx, pos_col, pos_row)
    d_qkv_p = swap_cores(d_qkv)

    def out_chunk(order, slot, incoming):
        v, order = chunk(order, slot, None, idx, ym, yp, ctx, ctx_p, incoming)
        return v if slot == SIDE - 1 else duo(v, "depth", 1), order

    def qkv_chunk(order, slot, sub, incoming):
        v, order = chunk(order, slot, sub, idx, xm, xp, d_qkv, d_qkv_p, incoming)
        return v if slot == SIDE - 1 else duo(v, "depth", 1), order

    term_m, order = input_terms(order, True, idx, d_qkv, w5, block)
    term_m = term_m.reshape(SIDE, SIDE, block, half)
    m = duo(term_m[1], "row", 1)
    out, order = out_chunk(order, 0, [])
    term_o, order = input_terms(order, False, idx, d_qkv, w5, block)
    o = duo(term_o[1], "col", 1)
    sub0, order = qkv_chunk(order, 0, 0, [])
    sub1, order = qkv_chunk(order, 0, 1, [])
    out, order = out_chunk(order, 1, [out])
    m, order = add(order, m, term_m, 2)
    m = duo(m, "row", 1)
    sub0, order = qkv_chunk(order, 1, 0, [sub0])
    o, order = add(order, o, term_o, 2)
    o = duo(o, "col", 1)
    sub1, order = qkv_chunk(order, 1, 1, [sub1])
    m, order = add(order, m, term_m, 3)
    m = duo(m, "row", 1)
    out, order = out_chunk(order, 2, [out])
    o, order = add(order, o, term_o, 3)
    o = duo(o, "col", 1)
    sub0, order = qkv_chunk(order, 2, 0, [sub0])
    m, order = add(order, m, term_m, 0)
    sub1, order = qkv_chunk(order, 2, 1, [sub1])
    o, order = add(order, o, term_o, 0)
    part_m, part_o = finish(m, "col"), finish(o, "row")
    d_wout, order = out_chunk(order, 3, [out])
    d_wqkv, order = qkv_chunk(order, 3, None, [sub0, sub1])
    d_tokens = jnp.where(
        core == 0,
        jnp.concatenate([part_m, part_o], axis=1),
        jnp.concatenate([part_o, part_m], axis=1),
    )[None]
    return (d_tokens, d_wqkv, d_wout)


def solution(mesh):
    in_specs = (
        P("depth", "col", "row"),
        P(None, None, ("row", "col")),
        P(("row", "col"), None),
        P("depth"),
        P("depth", "col", "row"),
    )
    out_specs = (
        P("depth", "col", "row"),
        P(None, "depth", ("row", "col")),
        P(("row", "col"), "depth"),
    )
    return jax.shard_map(body, mesh=mesh, in_specs=in_specs, out_specs=out_specs, check_vma=False)
```
